256 devices in a mesh: dp: 16 (over x, z_lo), ctx: 16 (over z_hi, y, core).
Axes of the slice: x: 4, y: 4, z: 8 (z_hi: 2, z_lo: 4; z = z_hi * 4 + z_lo), core: 2. Of those that a mesh axis runs over, the one named last changes fastest.
Arguments:
- query_rows: bfloat16 [16, 2048, 2560], P('dp', 'ctx'), may hold values from -8 to 8
- key_rows: bfloat16 [16, 2048, 512], P('dp', 'ctx'), may hold values from -8 to 8
- value_rows: bfloat16 [16, 2048, 512], P('dp', 'ctx'), may hold values from -6 to 6
- out_grad: bfloat16 [16, 2048, 2560], P('dp', 'ctx'), may hold values from -6 to 6
- doc_ids: int32 [16, 2048], P('dp', 'ctx'), may hold values from 0 to 7, never falling along the last dimension, each value on 1 to 1024 neighbouring positions
Outputs:
- query_grad: bfloat16 [16, 2048, 2560], P('dp', 'ctx')
- key_grad: bfloat16 [16, 2048, 512], P('dp', 'ctx')
- value_grad: bfloat16 [16, 2048, 512], P('dp', 'ctx')
- bias_grad: float32 [2560], replicated
The draws below stay inside these ranges and needn't reach their ends.
Inputs may be any that keep to these rules, and one draw needn't show every extreme that they name: `doc_ids`: each row numbers the 8 documents packed into one sequence in order, never falling; a document holds 1 to 1024 tokens and one holds exactly 1024.
All inputs are finite; a program needn't handle non-finite values.
Results may differ from the reference program's by a relative error of at most 0.03.
Values may be sent and summed in bfloat16 or wider, within the bound.
No kernel may reach another device: no remote copies, remote signals or barrier semaphores. Data moves between devices by JAX's collectives and lax.ppermute only.
A program may use at most 128 MiB of HBM per device.

```python
import math
import jax
import jax.numpy as jnp
import numpy as np
from jax import lax

HD = 128
QH = 20
KVH = 4
DOCS = 8
BATCH = 16
SEQ = 2048


def draw_query_rows(key, part):
    key = jax.random.fold_in(key, 5)
    normal_key = jax.random.fold_in(key, 0)
    drawn = 1.6 * jax.random.normal(normal_key, (BATCH, SEQ, QH * HD), jnp.float32)
    return jnp.clip(drawn, -8.0, 8.0).astype(jnp.bfloat16)


def draw_key_rows(key, part):
    key = jax.random.fold_in(key, 9)
    normal_key = jax.random.fold_in(key, 0)
    drawn = 1.6 * jax.random.normal(normal_key, (BATCH, SEQ, KVH * HD), jnp.float32)
    return jnp.clip(drawn, -8.0, 8.0).astype(jnp.bfloat16)


def levels(key, shape, pieces, least, high):
    def one(dim, parts):
        steps = jax.random.uniform(jax.random.fold_in(jax.random.fold_in(key, 6), dim), (parts,), jnp.float32, least / len(pieces), high / len(pieces))
        return jnp.repeat(jnp.exp(steps), shape[dim] // parts).reshape((-1,) + (1,) * (len(shape) - dim - 1))

    factor_of = one(*pieces[0])
    for cut in pieces[1:]:
        factor_of = factor_of * one(*cut)
    return factor_of


def profile(amount, total, bound, skew):
    weights = [(1 << 20) // math.isqrt(rank ** skew) + 1 for rank in range(2, amount + 1)]
    surplus, holding = total - bound - (amount - 1), [1] * (amount - 1)
    while surplus > 0:
        movable = [i for i in range(amount - 1) if holding[i] < bound]
        mass, left = sum([weights[i] for i in movable]), surplus
        for i in movable:
            addition = min(bound - holding[i], max(1, left * weights[i] // mass), surplus)
            holding[i] = holding[i] + addition
            surplus = surplus - addition
    return np.array([bound] + holding)


def uneven_parts(key, count, total, limit, slope):
    if count == 2:
        one = jax.random.randint(key, (), max(1, total - limit), min(limit, total - 1) + 1)
        return jnp.stack([one, total - one])
    lengths = jnp.asarray(profile(count, total, limit, slope), jnp.int32)
    pairs = (count - 1) // 2
    source_of, taker = lengths[1:1 + 2 * pairs:2], lengths[2:2 + 2 * pairs:2]
    margin = jnp.minimum(source_of - 1, limit - taker)
    passed = jax.random.randint(jax.random.fold_in(key, 1), (pairs,), 0, 1 << 20) % (margin + 1)
    lengths = lengths.at[1:1 + 2 * pairs:2].set(source_of - passed).at[2:2 + 2 * pairs:2].set(taker + passed)
    return lengths[jax.random.permutation(jax.random.fold_in(key, 2), count)]


def normal_values(own_key, dims, spread, reach, cuts=(), kind=jnp.bfloat16):
    array = jax.random.normal(own_key, dims, jnp.float32) * spread
    if len(cuts) > 0:
        array = levels(own_key, dims, cuts, -0.22, 0.18) * array
    return jnp.clip(array, min=-reach, max=reach).astype(kind)


def setup_inputs(seed: int = 0) -> dict:
    key_of = jax.random.split(jax.random.key(seed), 6)
    return {
        "query_rows": draw_query_rows(jax.random.fold_in(key_of[5], 71), 0),
        "key_rows": draw_key_rows(jax.random.fold_in(key_of[5], 71), 0),
        "value_rows": normal_values(key_of[2], (BATCH, SEQ, KVH * HD), 1.0, 6.0, ((0, 16), (1, 16))),
        "out_grad": normal_values(key_of[3], (BATCH, SEQ, QH * HD), 1.0, 6.0, ((0, 16), (1, 16))),
        "doc_ids": jax.vmap(lambda own: jnp.searchsorted(jnp.cumsum(uneven_parts(own, DOCS, SEQ, SEQ // 2, 2)), jnp.arange(SEQ), side="right"))(jax.random.split(key_of[4], BATCH)).reshape((BATCH, SEQ)).astype(jnp.int32),
    }


def head_grads(inputs):
    query_part, key_part, value_part, grad_part, docs = inputs
    inv_root = HD ** -0.5
    query_f = query_part.astype(jnp.float32)
    key_f = key_part.astype(jnp.float32)
    value_f = value_part.astype(jnp.float32)
    grad_f = grad_part.astype(jnp.float32)
    places = jnp.arange(SEQ, dtype=jnp.int32)
    allowed = (docs[:, None] == docs[None, :]) & (places[None, :] <= places[:, None])
    scores = jnp.einsum("igd,jd->gij", query_f, key_f) * inv_root
    row_max = jnp.max(jnp.where(allowed, scores, -1e30), axis=-1, keepdims=True)
    weights = jnp.where(allowed, jnp.exp(scores - row_max), 0.0)
    log_norm = row_max + jnp.log(jnp.sum(weights, axis=-1, keepdims=True))
    softmax = jnp.where(allowed, jnp.exp(scores - log_norm), 0.0)
    rounded = lax.optimization_barrier(softmax.astype(jnp.bfloat16)).astype(jnp.float32)
    attended = jnp.einsum("gij,jd->gid", rounded, value_f).astype(jnp.bfloat16)
    row_dots = jnp.einsum("gid,igd->gi", attended.astype(jnp.float32), grad_f)
    value_full = jnp.einsum("gij,igd->jd", rounded, grad_f)
    prob_grad = jnp.einsum("igd,jd->gij", grad_f, value_f)
    score_grad = softmax * (prob_grad - row_dots[..., None])
    score_round = lax.optimization_barrier(score_grad.astype(jnp.bfloat16)).astype(jnp.float32)
    query_full = jnp.einsum("gij,jd->igd", score_round, key_f) * inv_root
    key_full = jnp.einsum("gij,igd->jd", score_round, query_f) * inv_root
    return query_full, key_full, value_full


def reference(query_rows, key_rows, value_rows, out_grad, doc_ids):
    group_size = QH // KVH
    query_split = query_rows.reshape(BATCH, SEQ, KVH, group_size, HD).transpose(0, 2, 1, 3, 4).reshape(BATCH * KVH, SEQ, group_size, HD)
    grad_split = out_grad.reshape(BATCH, SEQ, KVH, group_size, HD).transpose(0, 2, 1, 3, 4).reshape(BATCH * KVH, SEQ, group_size, HD)
    key_split = key_rows.reshape(BATCH, SEQ, KVH, HD).transpose(0, 2, 1, 3).reshape(BATCH * KVH, SEQ, HD)
    value_split = value_rows.reshape(BATCH, SEQ, KVH, HD).transpose(0, 2, 1, 3).reshape(BATCH * KVH, SEQ, HD)
    doc_split = jnp.repeat(doc_ids, KVH, axis=0)
    query_full, key_full, value_full = lax.map(head_grads, (query_split, key_split, value_split, grad_split, doc_split))
    query_full = query_full.reshape(BATCH, KVH, SEQ, group_size, HD).transpose(0, 2, 1, 3, 4).reshape(BATCH, SEQ, QH * HD)
    key_full = key_full.reshape(BATCH, KVH, SEQ, HD).transpose(0, 2, 1, 3).reshape(BATCH, SEQ, KVH * HD)
    value_full = value_full.reshape(BATCH, KVH, SEQ, HD).transpose(0, 2, 1, 3).reshape(BATCH, SEQ, KVH * HD)
    bias_grad = jnp.sum(query_full, axis=(0, 1))
    return query_full.astype(jnp.bfloat16), key_full.astype(jnp.bfloat16), value_full.astype(jnp.bfloat16), bias_grad
```

```python
import math

import jax
import jax.numpy as jnp
from jax import lax
from jax.experimental import pallas as pl
from jax.experimental.pallas import tpu as pltpu
from jax.sharding import PartitionSpec as P

HD = 128
QH = 20
KVH = 4
GROUP = QH // KVH
ROWS = 128
PAIR = 2 * ROWS
HALF_Q = QH // 2 * HD
HALF_KV = KVH // 2 * HD
LINE = ROWS + 16
WINDOW = 5
INV_ROOT = HD ** (-0.5)
LOG2E = math.log2(math.e)
MASKED = -1e30


def place():
    index = lax.axis_index("ctx")
    return index // 8, (index // 2) % 4, index % 2


def pairs(target):
    out = []
    for z in range(2):
        for y in range(4):
            for c in range(2):
                to = target(z, y, c)
                if to is not None:
                    out.append((z * 8 + y * 2 + c, to[0] * 8 + to[1] * 2 + to[2]))
    return out


SWAP = pairs(lambda z, y, c: (z, y, 1 - c))
UP = pairs(lambda z, y, c: (1, y, c) if z == 0 else None)
DOWN = pairs(lambda z, y, c: (0, y, c) if z == 1 else None)
DOWN_CROSS = pairs(lambda z, y, c: (0, y, 1 - c) if z == 1 else None)


def near_pairs(k):
    return pairs(lambda z, y, c: (z, y + k, c) if y + k < 4 else None)


def far_pairs(k):
    return pairs(lambda z, y, c: (1, y - k, c) if z == 1 and y >= k else None)


def back_pairs(p):
    return pairs(
        lambda z, y, c: (z, (y + p) % 4, c) if z == 1 or y + p >= 4 else None
    )


def pack_kernel(q_ref, g_ref, k_ref, v_ref, ids_ref, send_ref, keep_ref, qg_ref):
    _, _, core = place()
    ids = jnp.broadcast_to(ids_ref[...].astype(jnp.float32), (16, ROWS)).astype(jnp.bfloat16)
    for ref, side in ((keep_ref, core), (send_ref, 1 - core)):
        columns = pl.ds(pl.multiple_of(side * HALF_KV, HALF_KV), HALF_KV)
        ref[0:ROWS, 0:HALF_KV] = k_ref[0, :, columns]
        ref[0:ROWS, HALF_KV:] = v_ref[0, :, columns]
        ref[ROWS:, 0:ROWS] = ids
        ref[ROWS:, ROWS:] = jnp.zeros((16, 2 * HALF_KV - ROWS), jnp.bfloat16)
    other = pl.ds(pl.multiple_of((1 - core) * HALF_Q, HALF_Q), HALF_Q)
    qg_ref[:, 0:HALF_Q] = q_ref[0, :, other]
    qg_ref[:, HALF_Q:] = g_ref[0, :, other]


def dot_nt(a, b):
    return lax.dot_general(a, b, (((1,), (1,)), ((), ())), preferred_element_type=jnp.float32)


def dot_nn(a, b):
    return jnp.dot(a, b, preferred_element_type=jnp.float32)


def attention_kernel(
    q_ref, g_ref, qg_ref, own, up, n1, n2, n3, f1, f2, f3,
    dq_keep, dq_send, bias_ref, d0, d1, d2, d3, d4,
    qs, gs, kv, kt, mask, top, s_ref, dp_ref, dk_acc, dv_acc,
):
    z, y, core = place()
    mine = pl.ds(pl.multiple_of(core * HALF_Q, HALF_Q), HALF_Q)
    qs[0:ROWS, :] = q_ref[0, :, mine]
    qs[ROWS:, :] = qg_ref[:, 0:HALF_Q]
    gs[0:ROWS, :] = g_ref[0, :, mine]
    gs[ROWS:, :] = qg_ref[:, HALF_Q:]

    own_ids = jnp.concatenate(
        [own[ROWS : ROWS + 8, 0:ROWS], own[LINE + ROWS : LINE + ROWS + 8, 0:ROWS]], axis=1
    ).astype(jnp.float32)
    first_doc = jnp.min(own_ids)
    q_ids = own_ids[0:1, :]

    def fill(p, ref):
        kv[p, 0:ROWS, :] = ref[0:ROWS, :]
        kv[p, ROWS:, :] = ref[LINE : LINE + ROWS, :]
        a = ref[ROWS : ROWS + 8, 0:ROWS].astype(jnp.float32)
        b = ref[LINE + ROWS : LINE + ROWS + 8, 0:ROWS].astype(jnp.float32)
        top[p] = jnp.maximum(jnp.max(a), jnp.max(b))
        for part, ids in enumerate((a, b)):
            column = jnp.broadcast_to(ids[0:1, :], (ROWS, ROWS)).T
            same = jnp.concatenate([column, column], axis=1) == q_ids
            rows = slice(part * ROWS, (part + 1) * ROWS)
            if p == WINDOW - 1:
                key_at = lax.broadcasted_iota(jnp.int32, (ROWS, PAIR), 0) + ROWS * (
                    core if part == 0 else 1 - core
                )
                lane = lax.broadcasted_iota(jnp.int32, (ROWS, PAIR), 1)
                own_at = lane + ROWS * core
                query_at = jnp.where(lane < ROWS, own_at, own_at - 2 * ROWS * core)
                same = same & (key_at <= query_at)
            mask[p, rows, :] = jnp.where(same, 0.0, MASKED)
        for head in range(2):
            block = kv[p, :, head * HD : (head + 1) * HD].astype(jnp.float32)
            kt[head, p] = block.T.astype(jnp.bfloat16)

    for p in range(WINDOW):
        top[p] = -1.0
    fill(WINDOW - 1, own)

    @pl.when(z == 1)
    def _():
        fill(0, up)

    for p, far, near in ((1, f1, n3), (2, f2, n2), (3, f3, n1)):

        @pl.when((y + p < 4) & (z == 1))
        def _():
            fill(p, far)

        @pl.when(y + p >= 4)
        def _():
            fill(p, near)

    count = jnp.int32(1)
    for p in range(WINDOW - 1):
        count = count + (top[p] >= first_doc).astype(jnp.int32)

    outs = (d0, d1, d2, d3, d4)

    def run(amount):
        blocks = range(WINDOW - amount, WINDOW)
        for p in range(WINDOW - amount):
            outs[p][...] = jnp.zeros(outs[p].shape, jnp.bfloat16)

        def kv_head(kh, _):
            key_columns = pl.ds(pl.multiple_of(kh * HD, HD), HD)
            value_columns = pl.ds(pl.multiple_of(HALF_KV + kh * HD, HD), HD)
            for p in blocks:
                dk_acc[p] = jnp.zeros((PAIR, HD), jnp.float32)
                dv_acc[p] = jnp.zeros((PAIR, HD), jnp.float32)

            def one(g, _):
                columns = pl.ds(pl.multiple_of((kh * GROUP + g) * HD, HD), HD)
                query, grad = qs[:, columns], gs[:, columns]
                peak = jnp.full((1, PAIR), MASKED, jnp.float32)
                for p in blocks:
                    scores = dot_nt(kv[p, :, key_columns], query) * (INV_ROOT * LOG2E) + mask[p]
                    s_ref[p] = scores
                    peak = jnp.maximum(peak, jnp.max(scores, axis=0, keepdims=True))
                    dp_ref[p] = dot_nt(kv[p, :, value_columns], grad)
                total = jnp.zeros((1, PAIR), jnp.float32)
                dots = jnp.zeros((1, PAIR), jnp.float32)
                for p in blocks:
                    weights = jnp.exp2(s_ref[p] - peak)
                    s_ref[p] = weights
                    total = total + jnp.sum(weights, axis=0, keepdims=True)
                    dots = dots + jnp.sum(weights * dp_ref[p], axis=0, keepdims=True)
                inverse = 1.0 / total
                dots = dots * inverse
                dq = jnp.zeros((HD, PAIR), jnp.float32)
                for p in blocks:
                    softmax = s_ref[p] * inverse
                    score_grad = (softmax * (dp_ref[p] - dots)).astype(jnp.bfloat16)
                    dv_acc[p] += dot_nn(softmax.astype(jnp.bfloat16), grad)
                    dk_acc[p] += dot_nn(score_grad, query)
                    dq = dq + dot_nn(kt[kh, p], score_grad)
                dq = dq.T * INV_ROOT
                bias_ref[0:1, columns] = jnp.sum(dq, axis=0, keepdims=True)
                dq_keep[:, columns] = dq[0:ROWS].astype(jnp.bfloat16)
                dq_send[:, columns] = dq[ROWS:].astype(jnp.bfloat16)
                return 0

            lax.fori_loop(0, GROUP, one, 0)
            for p in blocks:
                outs[p][:, key_columns] = (dk_acc[p] * INV_ROOT).astype(jnp.bfloat16)
                outs[p][:, value_columns] = dv_acc[p].astype(jnp.bfloat16)
            return 0

        lax.fori_loop(0, 2, kv_head, 0)

    for amount in range(1, WINDOW + 1):

        @pl.when(count == amount)
        def _():
            run(amount)


def move(array, table):
    return lax.ppermute(array, "ctx", table)


def body(query_rows, key_rows, value_rows, out_grad, doc_ids):
    z, y, core = place()
    bf16, f32 = jnp.bfloat16, jnp.float32
    shape = jax.ShapeDtypeStruct
    line = shape((LINE, 2 * HALF_KV), bf16)
    send, keep, qg = pl.pallas_call(
        pack_kernel, out_shape=(line, line, shape((ROWS, 2 * HALF_Q), bf16)), name="pack"
    )(query_rows, out_grad, key_rows, value_rows, doc_ids)
    own = jnp.concatenate([keep, move(send, SWAP)], axis=0)
    up = move(own, UP)
    near = [move(own, near_pairs(k)) for k in (1, 2, 3)]
    qg = move(qg, SWAP)
    far = [move(up, far_pairs(k)) for k in (1, 2, 3)]

    block = shape((PAIR, 2 * HALF_KV), bf16)
    outs = pl.pallas_call(
        attention_kernel,
        out_shape=(
            shape((ROWS, HALF_Q), bf16),
            shape((ROWS, HALF_Q), bf16),
            shape((1, HALF_Q), f32),
            *[block] * WINDOW,
        ),
        scratch_shapes=[
            pltpu.VMEM((PAIR, HALF_Q), bf16),
            pltpu.VMEM((PAIR, HALF_Q), bf16),
            pltpu.VMEM((WINDOW, PAIR, 2 * HALF_KV), bf16),
            pltpu.VMEM((2, WINDOW, HD, PAIR), bf16),
            pltpu.VMEM((WINDOW, PAIR, PAIR), f32),
            pltpu.SMEM((WINDOW,), f32),
            pltpu.VMEM((WINDOW, PAIR, PAIR), f32),
            pltpu.VMEM((WINDOW, PAIR, PAIR), f32),
            pltpu.VMEM((WINDOW, PAIR, HD), f32),
            pltpu.VMEM((WINDOW, PAIR, HD), f32),
        ],
        compiler_params=pltpu.CompilerParams(vmem_limit_bytes=40 * 1024 * 1024),
        name="attention",
    )(query_rows, out_grad, qg, own, up, *near, *far)
    dq_keep, dq_send, bias = outs[:3]
    parts = outs[3:]

    back = [move(parts[p], back_pairs(p)).astype(f32) for p in (1, 2, 3)]
    far_sum, near_sum = parts[0].astype(f32), parts[4].astype(f32)
    for p, got in zip((1, 2, 3), back):
        far_sum = far_sum + jnp.where(y >= p, got, 0.0)
        near_sum = near_sum + jnp.where(y >= p, 0.0, got)
    far_sum = far_sum.astype(bf16)
    same = move(far_sum[:ROWS], DOWN).astype(f32)
    cross = move(far_sum[ROWS:], DOWN_CROSS).astype(f32)
    swapped = move(near_sum[ROWS:].astype(bf16), SWAP).astype(f32)
    mine = (near_sum[:ROWS] + same).astype(bf16)
    theirs = (swapped + cross).astype(bf16)

    def join(a, b):
        return jnp.where(
            core == 0, jnp.concatenate([a, b], axis=1), jnp.concatenate([b, a], axis=1)
        )[None]

    key_out = join(mine[:, :HALF_KV], theirs[:, :HALF_KV])
    value_out = join(mine[:, HALF_KV:], theirs[:, HALF_KV:])
    query_out = join(dq_keep, move(dq_send, SWAP))

    bias = bias[0]
    for axis, first in (("ctx", 1), ("dp", 0)):
        size = lax.axis_size(axis)
        step = 1 << first
        while step < size:
            bias = bias + lax.ppermute(bias, axis, [(i, i ^ step) for i in range(size)])
            step *= 2
    other = move(bias, SWAP)
    bias_out = jnp.where(
        core == 0, jnp.concatenate([bias, other]), jnp.concatenate([other, bias])
    )
    return (query_out, key_out, value_out, bias_out)


def solution(mesh):
    in_specs = (
        P("dp", "ctx", None),
        P("dp", "ctx", None),
        P("dp", "ctx", None),
        P("dp", "ctx", None),
        P("dp", "ctx"),
    )
    out_specs = (P("dp", "ctx", None), P("dp", "ctx", None), P("dp", "ctx", None), P())
    return jax.shard_map(body, mesh=mesh, in_specs=in_specs, out_specs=out_specs, check_vma=False)
```

```python
import math

import jax
import jax.numpy as jnp
from jax import lax
from jax.experimental import pallas as pl
from jax.experimental.pallas import tpu as pltpu
from jax.sharding import PartitionSpec as P

HD = 128
QH = 20
KVH = 4
GROUP = QH // KVH
ROWS = 128
CHIPS = 4
GCOLS = GROUP * HD
LANES = GROUP * ROWS
LINE = ROWS + 16
BUNDLE = CHIPS * ROWS + 16
CHUNKS = 16
BLOCKS = 5
INV_ROOT = HD ** (-0.5)
LOG2E = math.log2(math.e)
MASKED = -1e30
bf16, f32 = jnp.bfloat16, jnp.float32


def place():
    index = lax.axis_index("ctx")
    return index // 8, (index // 2) % 4, index % 2


def pairs(target):
    out = []
    for z in range(2):
        for y in range(4):
            for c in range(2):
                to = target(z, y, c)
                if to is not None:
                    out.append((z * 8 + y * 2 + c, to[0] * 8 + to[1] * 2 + to[2]))
    return out


SWAP = pairs(lambda z, y, c: (z, y, 1 - c))
UP = pairs(lambda z, y, c: (1, y, c) if z == 0 else None)
DOWN = pairs(lambda z, y, c: (0, y, c) if z == 1 else None)


def shift(k):
    return pairs(lambda z, y, c: (z, (y + k) % CHIPS, c))


def head_of(y, k, width):
    return pl.ds(pl.multiple_of(lax.rem(y + k, CHIPS) * width, width), width)


def pack_kv_kernel(k_ref, v_ref, ids_ref, *outs):
    _, y, _ = place()
    ids = jnp.broadcast_to(ids_ref[...].astype(f32), (16, ROWS)).astype(bf16)
    for k, out in enumerate(outs):
        out[0:ROWS, 0:HD] = k_ref[0, :, head_of(y, k, HD)]
        out[0:ROWS, HD:] = v_ref[0, :, head_of(y, k, HD)]
        out[ROWS:, 0:HD] = ids
        out[ROWS:, HD:] = ids


def bundle_kernel(l0, l1, l2, l3, out):
    lines = (l0, l1, l2, l3)
    for k, line in enumerate(lines):
        out[k * ROWS : (k + 1) * ROWS, :] = line[0:ROWS, :]
    ids = [line[ROWS:, 0:HD].astype(f32)[0:8] for line in lines]
    first = jnp.concatenate([ids[0], ids[1]], axis=1)
    second = jnp.concatenate([ids[2], ids[3]], axis=1)
    out[CHIPS * ROWS :, :] = jnp.concatenate([first, second], axis=0).astype(bf16)


def pack_qg_kernel(q_ref, g_ref, after_ref, *outs):
    _, y, _ = place()
    for k, out in enumerate(outs):
        out[:, 0:GCOLS] = q_ref[0, :, head_of(y, k + 1, GCOLS)]
        out[:, GCOLS:] = g_ref[0, :, head_of(y, k + 1, GCOLS)]


def dot_nt(a, b):
    return lax.dot_general(a, b, (((1,), (1,)), ((), ())), preferred_element_type=f32)


def dot_nn(a, b):
    return jnp.dot(a, b, preferred_element_type=f32)


def ids_of(ref):
    rows = ref[CHIPS * ROWS :, :].astype(f32)
    return [rows[8 * (k // 2) : 8 * (k // 2) + 1, (k % 2) * ROWS : (k % 2 + 1) * ROWS] for k in range(4)]


def attention_kernel(
    q_ref, g_ref, g1, g2, g3, near_own, near_sib, far_own, far_sib,
    dq0, dq1, dq2, dq3, bias_ref, sib_ref, far_ref, near_ref,
    qs, gs, kv, kt, s_ref, dp_ref, peaks, dk_acc, dv_acc, dq_acc, starts, lows,
):
    z, y, core = place()

    for k, ref in enumerate((None, g1, g2, g3)):
        for h in range(GROUP):
            rows = slice(h * ROWS, (h + 1) * ROWS)
            if k == 0:
                columns = pl.ds(pl.multiple_of(y * GCOLS + h * HD, HD), HD)
                qs[k, rows, :] = q_ref[0, :, columns]
                gs[k, rows, :] = g_ref[0, :, columns]
            else:
                qs[k, rows, :] = ref[:, h * HD : (h + 1) * HD]
                gs[k, rows, :] = ref[:, GCOLS + h * HD : GCOLS + (h + 1) * HD]

    kv[0] = jnp.zeros((ROWS, 2 * HD), bf16)
    kt[0] = jnp.zeros((HD, ROWS), bf16)

    sources = ((far_own, 0, core), (far_sib, 0, 1 - core), (near_own, 1, core), (near_sib, 1, 1 - core))
    for ref, half, parity in sources:
        for k in range(CHIPS):
            at = 1 + half * 8 + 2 * lax.rem(y - k + CHIPS, CHIPS) + parity
            chunk = ref[k * ROWS : (k + 1) * ROWS, :]
            kv[at] = chunk
            kt[at] = chunk[:, 0:HD].astype(f32).T.astype(bf16)
    dk_acc[...] = jnp.zeros(dk_acc.shape, f32)
    dv_acc[...] = jnp.zeros(dv_acc.shape, f32)

    far_ids = [jnp.where(z == 1, row, -1.0) for ref in (far_own, far_sib) for row in ids_of(ref)]
    own_ids = ids_of(near_own)
    all_ids = jnp.concatenate(far_ids + own_ids + ids_of(near_sib), axis=0)
    begin = [jnp.sum((all_ids < d).astype(f32), keepdims=True).reshape(1, 1) for d in range(8)]
    for k in range(CHIPS):
        start = jnp.zeros((1, ROWS), f32)
        for d in range(8):
            start = start + jnp.where(own_ids[k] == d, begin[d], 0.0)
        starts[k] = jnp.broadcast_to(start, (8, ROWS)).astype(jnp.int32)
        lows[k] = jnp.min(start).astype(jnp.int32)

    def query_chunk(k, total_bias):
        place_in_half = 2 * lax.rem(y - k + CHIPS, CHIPS) + core
        here = 8 + place_in_half
        low = lows[k] // ROWS
        amount = (here - low + 2) // 2
        query, grad = qs[k], gs[k]
        start = starts[k][0:1, :]
        query_at = here * ROWS + lax.broadcasted_iota(jnp.int32, (1, ROWS), 1)

        def first(b, carried):
            peak, total, dots = carried
            base = here - 2 * b
            keys = kv[pl.ds(base, 2), :, 0:HD].reshape(2 * ROWS, HD)
            values = kv[pl.ds(base, 2), :, HD:].reshape(2 * ROWS, HD)
            key_at = (base - 1) * ROWS + lax.broadcasted_iota(jnp.int32, (2 * ROWS, ROWS), 0)
            allowed = (key_at >= start) & (key_at <= query_at)
            bias = jnp.where(allowed, 0.0, MASKED)
            bias = jnp.concatenate([bias] * GROUP, axis=1)
            scores = dot_nt(keys, query) * (INV_ROOT * LOG2E) + bias
            peak_now = jnp.maximum(peak, jnp.max(scores, axis=0, keepdims=True))
            weights = jnp.exp2(scores - peak_now)
            s_ref[b] = weights
            grads = dot_nt(values, grad)
            dp_ref[b] = grads
            peaks[b] = jnp.broadcast_to(peak_now, (8, LANES))
            fade = jnp.exp2(peak - peak_now)
            total = total * fade + jnp.sum(weights.reshape(-1, 8, LANES), axis=0)
            dots = dots * fade + jnp.sum((weights * grads).reshape(-1, 8, LANES), axis=0)
            return peak_now, total, dots

        nothing = jnp.zeros((8, LANES), f32)
        peak, total, dots = lax.fori_loop(
            0, amount, first, (jnp.full((1, LANES), MASKED, f32), nothing, nothing)
        )
        inverse = 1.0 / jnp.sum(total, axis=0, keepdims=True)
        dots = jnp.sum(dots, axis=0, keepdims=True) * inverse
        dq_acc[...] = jnp.zeros(dq_acc.shape, f32)

        def third(b, _):
            base = here - 2 * b
            softmax = s_ref[b] * (jnp.exp2(peaks[b][0:1] - peak) * inverse)
            score_grad = (softmax * (dp_ref[b] - dots)).astype(bf16)
            dv = dot_nn(softmax.astype(bf16), grad)
            dk = dot_nn(score_grad, query)
            dv_acc[pl.ds(base, 2)] += dv.reshape(2, ROWS, HD)
            dk_acc[pl.ds(base, 2)] += dk.reshape(2, ROWS, HD)
            dq_acc[...] += dot_nn(kt[base], score_grad[0:ROWS]) + dot_nn(
                kt[base + 1], score_grad[ROWS:]
            )
            return 0

        lax.fori_loop(0, amount, third, 0)
        bias_rows = []
        for h in range(GROUP):
            dq = dq_acc[:, h * ROWS : (h + 1) * ROWS].T * INV_ROOT
            bias_rows.append(jnp.sum(dq, axis=0, keepdims=True))
            for j, out in enumerate((dq0, dq1, dq2, dq3)):

                @pl.when(k == j)
                def _():
                    out[:, h * HD : (h + 1) * HD] = dq.astype(bf16)

        return total_bias + jnp.concatenate(bias_rows, axis=1)

    bias_ref[...] = lax.fori_loop(0, CHIPS, query_chunk, jnp.zeros((1, GCOLS), f32))

    half_rows = CHIPS * ROWS
    outputs = ((far_ref, 0, 0, core), (sib_ref, 0, 0, 1 - core), (near_ref, 0, 1, core), (sib_ref, half_rows, 1, 1 - core))
    for ref, offset, half, parity in outputs:
        for k in range(CHIPS):
            at = 1 + half * 8 + 2 * lax.rem(y - k + CHIPS, CHIPS) + parity
            rows = slice(offset + k * ROWS, offset + (k + 1) * ROWS)
            ref[rows, 0:HD] = (dk_acc[at] * INV_ROOT).astype(ref.dtype)
            ref[rows, HD:] = dv_acc[at].astype(ref.dtype)


def place_q_kernel(c0, c1, c2, c3, out):
    _, y, _ = place()
    for k, ref in enumerate((c0, c1, c2, c3)):
        out[0, :, head_of(y, k, GCOLS)] = ref[...]


def place_kernel(c0, c1, c2, c3, b0, b1, b2, b3, key_out, value_out, bias_out):
    _, y, _ = place()
    for k, ref in enumerate((c0, c1, c2, c3)):
        key_out[0, :, head_of(y, k, HD)] = ref[:, 0:HD]
        value_out[0, :, head_of(y, k, HD)] = ref[:, HD:]
    rows = [ref[...] for ref in (b0, b1, b2, b3)]
    for j in range(CHIPS):
        row = rows[j]
        for near in range(1, CHIPS):
            row = jnp.where(y == near, rows[(j - near) % CHIPS], row)
        bias_out[j * GCOLS : (j + 1) * GCOLS] = row


def move(array, table):
    return lax.ppermute(array, "ctx", table)


def meet(partner_x, partner_z):
    out = []
    for x in range(4):
        for z in range(8):
            px, pz = partner_x[x], partner_z[z]
            for rest in range(8):
                a = (x * 4 + z % 4) * 16 + z // 4 * 8 + rest
                b = (px * 4 + pz % 4) * 16 + pz // 4 * 8 + rest
                out.append((a, b))
    return out


STAY_X, STAY_Z = range(4), range(8)
MEETINGS = [
    meet((1, 0, 3, 2), STAY_Z),
    meet((3, 2, 1, 0), STAY_Z),
    meet(STAY_X, (1, 0, 3, 2, 5, 4, 7, 6)),
    meet(STAY_X, (7, 2, 1, 4, 3, 6, 5, 0)),
    meet(STAY_X, (3, 6, 5, 0, 7, 2, 1, 4)),
]


def body(query_rows, key_rows, value_rows, out_grad, doc_ids):
    _, y, _ = place()
    shape = jax.ShapeDtypeStruct
    vmem, anywhere = pl.BlockSpec(memory_space=pltpu.VMEM), pl.BlockSpec(memory_space=pl.ANY)

    lines = pl.pallas_call(
        pack_kv_kernel, out_shape=[shape((LINE, 2 * HD), bf16)] * CHIPS, name="pack_kv"
    )(key_rows, value_rows, doc_ids)
    lines = [lines[0]] + [move(lines[k], shift(k)) for k in (1, 2, 3)]
    near = pl.pallas_call(bundle_kernel, out_shape=shape((BUNDLE, 2 * HD), bf16), name="bundle")(
        *lines
    )
    far = move(near, UP)
    near_sib = move(near, SWAP)
    qg = pl.pallas_call(
        pack_qg_kernel,
        out_shape=[shape((ROWS, 2 * GCOLS), bf16)] * 3,
        in_specs=[vmem, vmem, anywhere],
        name="pack_qg",
    )(query_rows, out_grad, near)
    qg = [move(qg[k - 1], shift(k)) for k in (1, 2, 3)]
    far_sib = move(far, SWAP)

    half = shape((CHIPS * ROWS, 2 * HD), f32)
    outs = pl.pallas_call(
        attention_kernel,
        out_shape=(
            *[shape((ROWS, GCOLS), bf16)] * CHIPS,
            shape((1, GCOLS), f32),
            shape((2 * CHIPS * ROWS, 2 * HD), bf16),
            half,
            half,
        ),
        scratch_shapes=[
            pltpu.VMEM((CHIPS, LANES, HD), bf16),
            pltpu.VMEM((CHIPS, LANES, HD), bf16),
            pltpu.VMEM((CHUNKS + 1, ROWS, 2 * HD), bf16),
            pltpu.VMEM((CHUNKS + 1, HD, ROWS), bf16),
            pltpu.VMEM((BLOCKS, 2 * ROWS, LANES), f32),
            pltpu.VMEM((BLOCKS, 2 * ROWS, LANES), f32),
            pltpu.VMEM((BLOCKS, 8, LANES), f32),
            pltpu.VMEM((CHUNKS + 1, ROWS, HD), f32),
            pltpu.VMEM((CHUNKS + 1, ROWS, HD), f32),
            pltpu.VMEM((HD, LANES), f32),
            pltpu.VMEM((CHIPS, 8, ROWS), jnp.int32),
            pltpu.SMEM((CHIPS,), jnp.int32),
        ],
        compiler_params=pltpu.CompilerParams(vmem_limit_bytes=32 * 1024 * 1024),
        name="attention",
    )(query_rows, out_grad, *qg, near, near_sib, far, far_sib)
    dq, bias = outs[:CHIPS], outs[CHIPS][0]
    to_sib, far_part, near_part = outs[CHIPS + 1 :]

    sib = move(to_sib, SWAP).astype(f32)
    half_rows = CHIPS * ROWS
    far_sum = (far_part + sib[:half_rows]).astype(bf16)
    down = move(far_sum, DOWN)
    dq = [dq[0]] + [move(dq[k], shift(-k)) for k in (1, 2, 3)]
    kv_grad = (near_part + sib[half_rows:] + down.astype(f32)).astype(bf16)
    kv_grad = [kv_grad[k * ROWS : (k + 1) * ROWS] for k in range(CHIPS)]
    kv_grad = [kv_grad[0]] + [move(kv_grad[k], shift(-k)) for k in (1, 2, 3)]

    query_out = pl.pallas_call(
        place_q_kernel, out_shape=shape(query_rows.shape, bf16), name="place_q"
    )(*dq)

    bias = bias + move(bias, SWAP)
    bias = jnp.where(y < CHIPS, bias, far_sum[0, 0].astype(f32))
    for table in MEETINGS:
        bias = bias + lax.ppermute(bias, ("dp", "ctx"), table)
    heads = [bias] + [move(bias, shift(-k)) for k in (1, 2, 3)]
    key_out, value_out, bias_out = pl.pallas_call(
        place_kernel,
        out_shape=(
            shape(key_rows.shape, bf16),
            shape(value_rows.shape, bf16),
            shape((QH * HD,), f32),
        ),
        name="place",
    )(*kv_grad, *heads)
    return (query_out, key_out, value_out, bias_out)


def solution(mesh):
    in_specs = (
        P("dp", "ctx", None),
        P("dp", "ctx", None),
        P("dp", "ctx", None),
        P("dp", "ctx", None),
        P("dp", "ctx"),
    )
    out_specs = (P("dp", "ctx", None), P("dp", "ctx", None), P("dp", "ctx", None), P())
    return jax.shard_map(body, mesh=mesh, in_specs=in_specs, out_specs=out_specs, check_vma=False)
```

```python
import math

import jax
import jax.numpy as jnp
from jax import lax
from jax.experimental import pallas as pl
from jax.experimental.pallas import tpu as pltpu
from jax.sharding import PartitionSpec as P

HD = 128
QH = 20
KVH = 4
GROUP = QH // KVH
ROWS = 128
CHIPS = 4
GCOLS = GROUP * HD
LANES = GROUP * ROWS
LINE = ROWS + 16
BUNDLE = CHIPS * ROWS + 16
CHUNKS = 16
BLOCKS = 5
INV_ROOT = HD ** (-0.5)
LOG2E = math.log2(math.e)
MASKED = -1e30
bf16, f32 = jnp.bfloat16, jnp.float32


def place():
    index = lax.axis_index("ctx")
    return index // 8, (index // 2) % 4, index % 2


def pairs(target):
    out = []
    for z in range(2):
        for y in range(4):
            for c in range(2):
                to = target(z, y, c)
                if to is not None:
                    out.append((z * 8 + y * 2 + c, to[0] * 8 + to[1] * 2 + to[2]))
    return out


SWAP = pairs(lambda z, y, c: (z, y, 1 - c))
ACROSS = pairs(lambda z, y, c: (1 - z, y, c))


def shift(k):
    return pairs(lambda z, y, c: (z, (y + k) % CHIPS, c))


def head_of(y, k, width):
    return pl.ds(pl.multiple_of(lax.rem(y + k, CHIPS) * width, width), width)


def pack_kv_kernel(k_ref, v_ref, ids_ref, *outs):
    _, y, _ = place()
    ids = jnp.broadcast_to(ids_ref[...].astype(f32), (16, ROWS)).astype(bf16)
    for k, out in enumerate(outs):
        out[0:ROWS, 0:HD] = k_ref[0, :, head_of(y, k, HD)]
        out[0:ROWS, HD:] = v_ref[0, :, head_of(y, k, HD)]
        out[ROWS:, 0:HD] = ids
        out[ROWS:, HD:] = ids


def bundle_kernel(l0, l1, l2, l3, after_ref, out):
    lines = (l0, l1, l2, l3)
    for k, line in enumerate(lines):
        out[k * ROWS : (k + 1) * ROWS, :] = line[0:ROWS, :]
    ids = [line[ROWS:, 0:HD].astype(f32)[0:8] for line in lines]
    first = jnp.concatenate([ids[0], ids[1]], axis=1)
    second = jnp.concatenate([ids[2], ids[3]], axis=1)
    out[CHIPS * ROWS :, :] = jnp.concatenate([first, second], axis=0).astype(bf16)


def pack_qg_kernel(q_ref, g_ref, after_ref, *outs):
    _, y, _ = place()
    for k, out in enumerate(outs):
        out[:, 0:GCOLS] = q_ref[0, :, head_of(y, k + 1, GCOLS)]
        out[:, GCOLS:] = g_ref[0, :, head_of(y, k + 1, GCOLS)]


def dot_nt(a, b):
    return lax.dot_general(a, b, (((1,), (1,)), ((), ())), preferred_element_type=f32)


def dot_nn(a, b):
    return jnp.dot(a, b, preferred_element_type=f32)


def ids_of(ref):
    rows = ref[CHIPS * ROWS :, :].astype(f32)
    return [rows[8 * (k // 2) : 8 * (k // 2) + 1, (k % 2) * ROWS : (k % 2 + 1) * ROWS] for k in range(4)]


def attention_kernel(
    q_ref, g_ref, g1, g2, g3, near_own, near_sib, far_own, far_sib,
    dq0, dq1, dq2, dq3, bias_ref, sib_ref, far_ref, near_ref,
    qs, gs, kv, s_ref, dp_ref, peaks, dk_acc, dv_acc, dq_acc, starts, lows,
):
    z, y, core = place()

    for k, ref in enumerate((None, g1, g2, g3)):
        for h in range(GROUP):
            rows = slice(h * ROWS, (h + 1) * ROWS)
            if k == 0:
                columns = pl.ds(pl.multiple_of(y * GCOLS + h * HD, HD), HD)
                qs[k, rows, :] = q_ref[0, :, columns]
                gs[k, rows, :] = g_ref[0, :, columns]
            else:
                qs[k, rows, :] = ref[:, h * HD : (h + 1) * HD]
                gs[k, rows, :] = ref[:, GCOLS + h * HD : GCOLS + (h + 1) * HD]

    kv[0] = jnp.zeros((ROWS, 2 * HD), bf16)

    sources = ((far_own, 0, core), (far_sib, 0, 1 - core), (near_own, 1, core), (near_sib, 1, 1 - core))
    for ref, half, parity in sources:
        for k in range(CHIPS):
            at = 1 + half * 8 + 2 * lax.rem(y - k + CHIPS, CHIPS) + parity
            chunk = ref[k * ROWS : (k + 1) * ROWS, :]
            kv[at] = chunk
    dk_acc[...] = jnp.zeros(dk_acc.shape, f32)
    dv_acc[...] = jnp.zeros(dv_acc.shape, f32)

    far_ids = [jnp.where(z == 1, row, -1.0) for ref in (far_own, far_sib) for row in ids_of(ref)]
    own_ids = ids_of(near_own)
    all_ids = jnp.concatenate(far_ids + own_ids + ids_of(near_sib), axis=0)
    begin = [jnp.sum((all_ids < d).astype(f32), keepdims=True).reshape(1, 1) for d in range(8)]
    for k in range(CHIPS):
        start = jnp.zeros((1, ROWS), f32)
        for d in range(8):
            start = start + jnp.where(own_ids[k] == d, begin[d], 0.0)
        starts[k] = jnp.broadcast_to(start, (8, ROWS)).astype(jnp.int32)
        lows[k] = jnp.min(start).astype(jnp.int32)

    def query_chunk(k, total_bias):
        place_in_half = 2 * lax.rem(y - k + CHIPS, CHIPS) + core
        here = 8 + place_in_half
        low = lows[k] // ROWS
        amount = (here - low + 2) // 2
        query, grad = qs[k], gs[k]
        start = starts[k][0:1, :]
        query_at = here * ROWS + lax.broadcasted_iota(jnp.int32, (1, ROWS), 1)

        def first(b, carried):
            peak, total, dots = carried
            base = here - 2 * b
            keys = kv[pl.ds(base, 2), :, 0:HD].reshape(2 * ROWS, HD)
            values = kv[pl.ds(base, 2), :, HD:].reshape(2 * ROWS, HD)
            key_at = (base - 1) * ROWS + lax.broadcasted_iota(jnp.int32, (2 * ROWS, ROWS), 0)
            allowed = (key_at >= start) & (key_at <= query_at)
            bias = jnp.where(allowed, 0.0, MASKED)
            bias = jnp.concatenate([bias] * GROUP, axis=1)
            scores = dot_nt(keys, query) * (INV_ROOT * LOG2E) + bias
            peak_now = jnp.maximum(peak, jnp.max(scores, axis=0, keepdims=True))
            weights = jnp.exp2(scores - peak_now)
            s_ref[b] = weights
            grads = dot_nt(values, grad)
            dp_ref[b] = grads
            peaks[b] = jnp.broadcast_to(peak_now, (8, LANES))
            fade = jnp.exp2(peak - peak_now)
            total = total * fade + jnp.sum(weights.reshape(-1, 8, LANES), axis=0)
            dots = dots * fade + jnp.sum((weights * grads).reshape(-1, 8, LANES), axis=0)
            return peak_now, total, dots

        nothing = jnp.zeros((8, LANES), f32)
        peak, total, dots = lax.fori_loop(
            0, amount, first, (jnp.full((1, LANES), MASKED, f32), nothing, nothing)
        )
        inverse = 1.0 / jnp.sum(total, axis=0, keepdims=True)
        dots = jnp.sum(dots, axis=0, keepdims=True) * inverse
        dq_acc[...] = jnp.zeros(dq_acc.shape, f32)

        def third(b, _):
            base = here - 2 * b
            softmax = s_ref[b] * (jnp.exp2(peaks[b][0:1] - peak) * inverse)
            score_grad = (softmax * (dp_ref[b] - dots)).astype(bf16)
            dv = dot_nn(softmax.astype(bf16), grad)
            dk = dot_nn(score_grad, query)
            dv_acc[pl.ds(base, 2)] += dv.reshape(2, ROWS, HD)
            dk_acc[pl.ds(base, 2)] += dk.reshape(2, ROWS, HD)
            keys = kv[pl.ds(base, 2), :, 0:HD].reshape(2 * ROWS, HD)
            dq_acc[...] += lax.dot_general(score_grad, keys, (((0,), (0,)), ((), ())), preferred_element_type=f32)
            return 0

        lax.fori_loop(0, amount, third, 0)
        bias_rows = []
        for h in range(GROUP):
            dq = dq_acc[h * ROWS : (h + 1) * ROWS] * INV_ROOT
            bias_rows.append(jnp.sum(dq, axis=0, keepdims=True))
            for j, out in enumerate((dq0, dq1, dq2, dq3)):

                @pl.when(k == j)
                def _():
                    out[:, h * HD : (h + 1) * HD] = dq.astype(bf16)

        return total_bias + jnp.concatenate(bias_rows, axis=1)

    bias_ref[...] = lax.fori_loop(0, CHIPS, query_chunk, jnp.zeros((1, GCOLS), f32))

    half_rows = CHIPS * ROWS
    outputs = ((far_ref, 0, 0, core), (sib_ref, 0, 0, 1 - core), (near_ref, 0, 1, core), (sib_ref, half_rows, 1, 1 - core))
    for ref, offset, half, parity in outputs:
        for k in range(CHIPS):
            at = 1 + half * 8 + 2 * lax.rem(y - k + CHIPS, CHIPS) + parity
            rows = slice(offset + k * ROWS, offset + (k + 1) * ROWS)
            ref[rows, 0:HD] = (dk_acc[at] * INV_ROOT).astype(ref.dtype)
            ref[rows, HD:] = dv_acc[at].astype(ref.dtype)


def place_q_kernel(c0, c1, c2, c3, out):
    _, y, _ = place()
    for k, ref in enumerate((c0, c1, c2, c3)):
        out[0, :, head_of(y, k, GCOLS)] = ref[...]


def place_kernel(c0, c1, c2, c3, b0, b1, b2, b3, key_out, value_out, bias_out):
    _, y, _ = place()
    for k, ref in enumerate((c0, c1, c2, c3)):
        key_out[0, :, head_of(y, k, HD)] = ref[:, 0:HD]
        value_out[0, :, head_of(y, k, HD)] = ref[:, HD:]
    rows = [ref[...] for ref in (b0, b1, b2, b3)]
    for j in range(CHIPS):
        row = rows[j]
        for near in range(1, CHIPS):
            row = jnp.where(y == near, rows[(j - near) % CHIPS], row)
        bias_out[j * GCOLS : (j + 1) * GCOLS] = row


def move(array, table):
    return lax.ppermute(array, "ctx", table)


def meet(partner_x, partner_z):
    out = []
    for x in range(4):
        for z in range(8):
            px, pz = partner_x[x], partner_z[z]
            for rest in range(8):
                a = (x * 4 + z % 4) * 16 + z // 4 * 8 + rest
                b = (px * 4 + pz % 4) * 16 + pz // 4 * 8 + rest
                out.append((a, b))
    return out


STAY_X, STAY_Z = range(4), range(8)
MEETINGS = [
    meet((1, 0, 3, 2), STAY_Z),
    meet((3, 2, 1, 0), STAY_Z),
    meet(STAY_X, (1, 0, 3, 2, 5, 4, 7, 6)),
    meet(STAY_X, (7, 2, 1, 4, 3, 6, 5, 0)),
    meet(STAY_X, (3, 6, 5, 0, 7, 2, 1, 4)),
]


def body(query_rows, key_rows, value_rows, out_grad, doc_ids):
    _, y, _ = place()
    shape = jax.ShapeDtypeStruct
    vmem, anywhere = pl.BlockSpec(memory_space=pltpu.VMEM), pl.BlockSpec(memory_space=pl.ANY)

    lines = pl.pallas_call(
        pack_kv_kernel, out_shape=[shape((LINE, 2 * HD), bf16)] * CHIPS, name="pack_kv"
    )(key_rows, value_rows, doc_ids)
    qg = pl.pallas_call(
        pack_qg_kernel,
        out_shape=[shape((ROWS, 2 * GCOLS), bf16)] * 3,
        in_specs=[vmem, vmem, anywhere],
        name="pack_qg",
    )(query_rows, out_grad, lines[0])
    lines = [lines[0]] + [move(lines[k], shift(k)) for k in (1, 2, 3)]
    near = pl.pallas_call(
        bundle_kernel,
        out_shape=shape((BUNDLE, 2 * HD), bf16),
        in_specs=[vmem] * 4 + [anywhere],
        name="bundle",
    )(*lines, qg[0])
    far = move(near, ACROSS)
    near_sib = move(near, SWAP)
    qg = [move(qg[k - 1], shift(k)) for k in (1, 2, 3)]
    far_sib = move(far, SWAP)

    half = shape((CHIPS * ROWS, 2 * HD), f32)
    outs = pl.pallas_call(
        attention_kernel,
        out_shape=(
            *[shape((ROWS, GCOLS), bf16)] * CHIPS,
            shape((1, GCOLS), f32),
            shape((2 * CHIPS * ROWS, 2 * HD), bf16),
            half,
            half,
        ),
        scratch_shapes=[
            pltpu.VMEM((CHIPS, LANES, HD), bf16),
            pltpu.VMEM((CHIPS, LANES, HD), bf16),
            pltpu.VMEM((CHUNKS + 1, ROWS, 2 * HD), bf16),
            pltpu.VMEM((BLOCKS, 2 * ROWS, LANES), f32),
            pltpu.VMEM((BLOCKS, 2 * ROWS, LANES), f32),
            pltpu.VMEM((BLOCKS, 8, LANES), f32),
            pltpu.VMEM((CHUNKS + 1, ROWS, HD), f32),
            pltpu.VMEM((CHUNKS + 1, ROWS, HD), f32),
            pltpu.VMEM((LANES, HD), f32),
            pltpu.VMEM((CHIPS, 8, ROWS), jnp.int32),
            pltpu.SMEM((CHIPS,), jnp.int32),
        ],
        compiler_params=pltpu.CompilerParams(vmem_limit_bytes=24 * 1024 * 1024),
        name="attention",
    )(query_rows, out_grad, *qg, near, near_sib, far, far_sib)
    dq, bias = outs[:CHIPS], outs[CHIPS][0]
    to_sib, far_part, near_part = outs[CHIPS + 1 :]

    sib = move(to_sib, SWAP).astype(f32)
    half_rows = CHIPS * ROWS
    far_sum = (far_part + sib[:half_rows]).astype(bf16)
    down = move(far_sum, ACROSS)
    dq = [dq[0]] + [move(dq[k], shift(-k)) for k in (1, 2, 3)]
    kv_grad = (near_part + sib[half_rows:] + down.astype(f32)).astype(bf16)
    kv_grad = [kv_grad[k * ROWS : (k + 1) * ROWS] for k in range(CHIPS)]
    kv_grad = [kv_grad[0]] + [move(kv_grad[k], shift(-k)) for k in (1, 2, 3)]

    query_out = pl.pallas_call(
        place_q_kernel, out_shape=shape(query_rows.shape, bf16), name="place_q"
    )(*dq)

    bias = bias + move(bias, SWAP)
    bias = jnp.where(y < CHIPS, bias, far_sum[0, 0].astype(f32))
    for table in MEETINGS:
        bias = bias + lax.ppermute(bias, ("dp", "ctx"), table)
    heads = [bias] + [move(bias, shift(-k)) for k in (1, 2, 3)]
    key_out, value_out, bias_out = pl.pallas_call(
        place_kernel,
        out_shape=(
            shape(key_rows.shape, bf16),
            shape(value_rows.shape, bf16),
            shape((QH * HD,), f32),
        ),
        name="place",
    )(*kv_grad, *heads)
    return (query_out, key_out, value_out, bias_out)


def solution(mesh):
    in_specs = (
        P("dp", "ctx", None),
        P("dp", "ctx", None),
        P("dp", "ctx", None),
        P("dp", "ctx", None),
        P("dp", "ctx"),
    )
    out_specs = (P("dp", "ctx", None), P("dp", "ctx", None), P("dp", "ctx", None), P())
    return jax.shard_map(body, mesh=mesh, in_specs=in_specs, out_specs=out_specs, check_vma=False)
```

```python
import math

import jax
import jax.numpy as jnp
from jax import lax
from jax.experimental import pallas as pl
from jax.experimental.pallas import tpu as pltpu
from jax.sharding import PartitionSpec as P

HD = 128
QH = 20
KVH = 4
GROUP = QH // KVH
ROWS = 128
CHIPS = 4
GCOLS = GROUP * HD
LANES = GROUP * ROWS
LINE = ROWS + 16
BUNDLE = CHIPS * ROWS + 16
CHUNKS = 16
BLOCKS = 5
INV_ROOT = HD ** (-0.5)
LOG2E = math.log2(math.e)
MASKED = -1e30
bf16, f32 = jnp.bfloat16, jnp.float32


def place():
    index = lax.axis_index("ctx")
    return index // 8, (index // 2) % 4, index % 2


def pairs(target):
    out = []
    for z in range(2):
        for y in range(4):
            for c in range(2):
                to = target(z, y, c)
                if to is not None:
                    out.append((z * 8 + y * 2 + c, to[0] * 8 + to[1] * 2 + to[2]))
    return out


SWAP = pairs(lambda z, y, c: (z, y, 1 - c))
ACROSS = pairs(lambda z, y, c: (1 - z, y, c))


def shift(k):
    return pairs(lambda z, y, c: (z, (y + k) % CHIPS, c))


def head_of(y, k, width):
    return pl.ds(pl.multiple_of(lax.rem(y + k, CHIPS) * width, width), width)


def pack_kv_kernel(k_ref, v_ref, ids_ref, *outs):
    _, y, _ = place()
    ids = jnp.broadcast_to(ids_ref[...].astype(f32), (16, ROWS)).astype(bf16)
    for k, out in enumerate(outs):
        out[0:ROWS, 0:HD] = k_ref[0, :, head_of(y, k, HD)]
        out[0:ROWS, HD:] = v_ref[0, :, head_of(y, k, HD)]
        out[ROWS:, 0:HD] = ids
        out[ROWS:, HD:] = ids


def bundle_kernel(l0, l1, l2, l3, after_ref, out):
    lines = (l0, l1, l2, l3)
    for k, line in enumerate(lines):
        out[k * ROWS : (k + 1) * ROWS, :] = line[0:ROWS, :]
    ids = [line[ROWS:, 0:HD].astype(f32)[0:8] for line in lines]
    first = jnp.concatenate([ids[0], ids[1]], axis=1)
    second = jnp.concatenate([ids[2], ids[3]], axis=1)
    out[CHIPS * ROWS :, :] = jnp.concatenate([first, second], axis=0).astype(bf16)


def pack_qg_kernel(q_ref, g_ref, after_ref, *outs):
    _, y, _ = place()
    for k, out in enumerate(outs):
        out[:, 0:GCOLS] = q_ref[0, :, head_of(y, k, GCOLS)]
        out[:, GCOLS:] = g_ref[0, :, head_of(y, k, GCOLS)]


def dot_nt(a, b):
    return lax.dot_general(a, b, (((1,), (1,)), ((), ())), preferred_element_type=f32)


def dot_nn(a, b):
    return jnp.dot(a, b, preferred_element_type=f32)


def ids_of(ref):
    rows = ref[CHIPS * ROWS :, :].astype(f32)
    return [rows[8 * (k // 2) : 8 * (k // 2) + 1, (k % 2) * ROWS : (k % 2 + 1) * ROWS] for k in range(4)]


def attention_kernel(
    g0, g1, g2, g3, near_own, near_sib, far_own, far_sib,
    dq0, dq1, dq2, dq3, bias_ref, sib_ref, far_ref, near_ref,
    qs, gs, kv, s_ref, dp_ref, peaks, dk_acc, dv_acc, dq_acc, starts, lows,
):
    z, y, core = place()

    for k, ref in enumerate((g0, g1, g2, g3)):
        for h in range(GROUP):
            rows = slice(h * ROWS, (h + 1) * ROWS)
            qs[k, rows, :] = ref[:, h * HD : (h + 1) * HD]
            gs[k, rows, :] = ref[:, GCOLS + h * HD : GCOLS + (h + 1) * HD]

    kv[0] = jnp.zeros((ROWS, 2 * HD), bf16)

    sources = ((far_own, 0, core), (far_sib, 0, 1 - core), (near_own, 1, core), (near_sib, 1, 1 - core))
    for ref, half, parity in sources:
        for k in range(CHIPS):
            at = 1 + half * 8 + 2 * lax.rem(y - k + CHIPS, CHIPS) + parity
            chunk = ref[k * ROWS : (k + 1) * ROWS, :]
            kv[at] = chunk
    dk_acc[...] = jnp.zeros(dk_acc.shape, f32)
    dv_acc[...] = jnp.zeros(dv_acc.shape, f32)

    far_ids = [jnp.where(z == 1, row, -1.0) for ref in (far_own, far_sib) for row in ids_of(ref)]
    own_ids = ids_of(near_own)
    all_ids = jnp.concatenate(far_ids + own_ids + ids_of(near_sib), axis=0)
    begin = [jnp.sum((all_ids < d).astype(f32), keepdims=True).reshape(1, 1) for d in range(8)]
    for k in range(CHIPS):
        start = jnp.zeros((1, ROWS), f32)
        for d in range(8):
            start = start + jnp.where(own_ids[k] == d, begin[d], 0.0)
        starts[k] = jnp.broadcast_to(start, (8, ROWS)).astype(jnp.int32)
        lows[k] = jnp.min(start).astype(jnp.int32)

    def query_chunk(k, total_bias):
        place_in_half = 2 * lax.rem(y - k + CHIPS, CHIPS) + core
        here = 8 + place_in_half
        low = lows[k] // ROWS
        count = here - low + 1
        full, odd = count // 2, lax.rem(count, 2) == 1
        query, grad = qs[k], gs[k]
        start = starts[k][0:1, :]
        query_at = here * ROWS + lax.broadcasted_iota(jnp.int32, (1, ROWS), 1)

        def first(b, base, chunks, carried):
            peak, total, dots = carried
            size = chunks * ROWS
            keys = kv[pl.ds(base, chunks), :, 0:HD].reshape(size, HD)
            values = kv[pl.ds(base, chunks), :, HD:].reshape(size, HD)
            key_at = (base - 1) * ROWS + lax.broadcasted_iota(jnp.int32, (size, ROWS), 0)
            allowed = (key_at >= start) & (key_at <= query_at)
            bias = jnp.where(allowed, 0.0, MASKED)
            bias = jnp.concatenate([bias] * GROUP, axis=1)
            scores = dot_nt(keys, query) * (INV_ROOT * LOG2E) + bias
            peak_now = jnp.maximum(peak, jnp.max(scores, axis=0, keepdims=True))
            weights = jnp.exp2(scores - peak_now)
            s_ref[b, 0:size] = weights
            grads = dot_nt(values, grad)
            dp_ref[b, 0:size] = grads
            peaks[b] = jnp.broadcast_to(peak_now, (8, LANES))
            fade = jnp.exp2(peak - peak_now)
            total = total * fade + jnp.sum(weights.reshape(-1, 8, LANES), axis=0)
            dots = dots * fade + jnp.sum((weights * grads).reshape(-1, 8, LANES), axis=0)
            return peak_now, total, dots

        nothing = jnp.zeros((8, LANES), f32)
        carried = lax.fori_loop(
            0,
            full,
            lambda b, carried: first(b, here - 2 * b, 2, carried),
            (jnp.full((1, LANES), MASKED, f32), nothing, nothing),
        )
        peak, total, dots = lax.cond(
            odd, lambda c: first(full, low + 1, 1, c), lambda c: c, carried
        )
        inverse = 1.0 / jnp.sum(total, axis=0, keepdims=True)
        dots = jnp.sum(dots, axis=0, keepdims=True) * inverse
        dq_acc[...] = jnp.zeros(dq_acc.shape, f32)

        def third(b, base, chunks):
            size = chunks * ROWS
            softmax = s_ref[b, 0:size] * (jnp.exp2(peaks[b][0:1] - peak) * inverse)
            score_grad = (softmax * (dp_ref[b, 0:size] - dots)).astype(bf16)
            dv = dot_nn(softmax.astype(bf16), grad)
            dk = dot_nn(score_grad, query)
            dv_acc[pl.ds(base, chunks)] += dv.reshape(chunks, ROWS, HD)
            dk_acc[pl.ds(base, chunks)] += dk.reshape(chunks, ROWS, HD)
            keys = kv[pl.ds(base, chunks), :, 0:HD].reshape(size, HD)
            dq_acc[...] += lax.dot_general(
                score_grad, keys, (((0,), (0,)), ((), ())), preferred_element_type=f32
            )

        @pl.loop(0, full)
        def _(b):
            third(b, here - 2 * b, 2)

        @pl.when(odd)
        def _():
            third(full, low + 1, 1)

        bias_rows = []
        for h in range(GROUP):
            dq = dq_acc[h * ROWS : (h + 1) * ROWS] * INV_ROOT
            bias_rows.append(jnp.sum(dq, axis=0, keepdims=True))
            for j, out in enumerate((dq0, dq1, dq2, dq3)):

                @pl.when(k == j)
                def _():
                    out[:, h * HD : (h + 1) * HD] = dq.astype(bf16)

        bias_rows.append(jnp.zeros((8 - GROUP, HD), f32))
        return total_bias + jnp.concatenate(bias_rows, axis=0)

    bias = lax.fori_loop(0, CHIPS, query_chunk, jnp.zeros((8, HD), f32))
    bias_ref[...] = bias
    high = bias.astype(bf16).astype(f32)
    middle = (bias - high).astype(bf16).astype(f32)
    low_part = bias - high - middle
    terms = jnp.concatenate([high, middle], axis=1), jnp.concatenate([low_part, low_part * 0], axis=1)
    sib_ref[2 * CHIPS * ROWS :, :] = jnp.concatenate(terms, axis=0).astype(bf16)

    half_rows = CHIPS * ROWS
    outputs = ((far_ref, 0, 0, core), (sib_ref, 0, 0, 1 - core), (near_ref, 0, 1, core), (sib_ref, half_rows, 1, 1 - core))
    for ref, offset, half, parity in outputs:
        for k in range(CHIPS):
            at = 1 + half * 8 + 2 * lax.rem(y - k + CHIPS, CHIPS) + parity
            rows = slice(offset + k * ROWS, offset + (k + 1) * ROWS)
            ref[rows, 0:HD] = (dk_acc[at] * INV_ROOT).astype(ref.dtype)
            ref[rows, HD:] = dv_acc[at].astype(ref.dtype)


def place_q_kernel(c0, c1, c2, c3, out):
    _, y, _ = place()
    for k, ref in enumerate((c0, c1, c2, c3)):
        out[0, :, head_of(y, k, GCOLS)] = ref[...]


def place_kernel(c0, c1, c2, c3, b0, b1, b2, b3, key_out, value_out, bias_out):
    _, y, _ = place()
    for k, ref in enumerate((c0, c1, c2, c3)):
        key_out[0, :, head_of(y, k, HD)] = ref[:, 0:HD]
        value_out[0, :, head_of(y, k, HD)] = ref[:, HD:]
    rows = [ref[...] for ref in (b0, b1, b2, b3)]
    for j in range(CHIPS):
        row = rows[j]
        for near in range(1, CHIPS):
            row = jnp.where(y == near, rows[(j - near) % CHIPS], row)
        for h in range(GROUP):
            at = j * GCOLS + h * HD
            bias_out[at : at + HD] = row[h]


def move(array, table):
    return lax.ppermute(array, "ctx", table)


def meet(partner_x, partner_z):
    out = []
    for x in range(4):
        for z in range(8):
            px, pz = partner_x[x], partner_z[z]
            for rest in range(8):
                a = (x * 4 + z % 4) * 16 + z // 4 * 8 + rest
                b = (px * 4 + pz % 4) * 16 + pz // 4 * 8 + rest
                out.append((a, b))
    return out


STAY_X, STAY_Z = range(4), range(8)
MEETINGS = [
    meet((1, 0, 3, 2), STAY_Z),
    meet((3, 2, 1, 0), STAY_Z),
    meet(STAY_X, (1, 0, 3, 2, 5, 4, 7, 6)),
    meet(STAY_X, (7, 2, 1, 4, 3, 6, 5, 0)),
    meet(STAY_X, (3, 6, 5, 0, 7, 2, 1, 4)),
]


def body(query_rows, key_rows, value_rows, out_grad, doc_ids):
    _, y, _ = place()
    shape = jax.ShapeDtypeStruct
    vmem, anywhere = pl.BlockSpec(memory_space=pltpu.VMEM), pl.BlockSpec(memory_space=pl.ANY)

    lines = pl.pallas_call(
        pack_kv_kernel, out_shape=[shape((LINE, 2 * HD), bf16)] * CHIPS, name="pack_kv"
    )(key_rows, value_rows, doc_ids)
    qg = pl.pallas_call(
        pack_qg_kernel,
        out_shape=[shape((ROWS, 2 * GCOLS), bf16)] * CHIPS,
        in_specs=[vmem, vmem, anywhere],
        name="pack_qg",
    )(query_rows, out_grad, lines[0])
    lines = [lines[0]] + [move(lines[k], shift(k)) for k in (1, 2, 3)]
    near = pl.pallas_call(
        bundle_kernel,
        out_shape=shape((BUNDLE, 2 * HD), bf16),
        in_specs=[vmem] * 4 + [anywhere],
        name="bundle",
    )(*lines, qg[0])
    far = move(near, ACROSS)
    near_sib = move(near, SWAP)
    qg = [qg[0]] + [move(qg[k], shift(k)) for k in (1, 2, 3)]
    far_sib = move(far, SWAP)

    half = shape((CHIPS * ROWS, 2 * HD), f32)
    outs = pl.pallas_call(
        attention_kernel,
        out_shape=(
            *[shape((ROWS, GCOLS), bf16)] * CHIPS,
            shape((8, HD), f32),
            shape((2 * CHIPS * ROWS + 16, 2 * HD), bf16),
            half,
            half,
        ),
        scratch_shapes=[
            pltpu.VMEM((CHIPS, LANES, HD), bf16),
            pltpu.VMEM((CHIPS, LANES, HD), bf16),
            pltpu.VMEM((CHUNKS + 1, ROWS, 2 * HD), bf16),
            pltpu.VMEM((BLOCKS, 2 * ROWS, LANES), f32),
            pltpu.VMEM((BLOCKS, 2 * ROWS, LANES), f32),
            pltpu.VMEM((BLOCKS, 8, LANES), f32),
            pltpu.VMEM((CHUNKS + 1, ROWS, HD), f32),
            pltpu.VMEM((CHUNKS + 1, ROWS, HD), f32),
            pltpu.VMEM((LANES, HD), f32),
            pltpu.VMEM((CHIPS, 8, ROWS), jnp.int32),
            pltpu.SMEM((CHIPS,), jnp.int32),
        ],
        compiler_params=pltpu.CompilerParams(vmem_limit_bytes=36 * 1024 * 1024),
        name="attention",
    )(*qg, near, near_sib, far, far_sib)
    dq, bias = outs[:CHIPS], outs[CHIPS]
    to_sib, far_part, near_part = outs[CHIPS + 1 :]

    sib = move(to_sib, SWAP)
    half_rows = CHIPS * ROWS
    far_sum = (far_part + sib[:half_rows].astype(f32)).astype(bf16)
    down = move(far_sum, ACROSS)
    dq = [dq[0]] + [move(dq[k], shift(-k)) for k in (1, 2, 3)]
    kv_grad = (near_part + sib[half_rows : 2 * half_rows].astype(f32) + down.astype(f32)).astype(bf16)
    kv_grad = [kv_grad[k * ROWS : (k + 1) * ROWS] for k in range(CHIPS)]
    kv_grad = [kv_grad[0]] + [move(kv_grad[k], shift(-k)) for k in (1, 2, 3)]

    query_out = pl.pallas_call(
        place_q_kernel, out_shape=shape(query_rows.shape, bf16), name="place_q"
    )(*dq)

    terms = sib[2 * half_rows :].astype(f32)
    bias = bias + ((terms[0:8, 0:HD] + terms[0:8, HD:]) + terms[8:, 0:HD])
    for table in MEETINGS:
        bias = bias + lax.ppermute(bias, ("dp", "ctx"), table)
    heads = [bias] + [move(bias, shift(-k)) for k in (1, 2, 3)]
    key_out, value_out, bias_out = pl.pallas_call(
        place_kernel,
        out_shape=(
            shape(key_rows.shape, bf16),
            shape(value_rows.shape, bf16),
            shape((QH * HD,), f32),
        ),
        name="place",
    )(*kv_grad, *heads)
    return (query_out, key_out, value_out, bias_out)


def solution(mesh):
    in_specs = (
        P("dp", "ctx", None),
        P("dp", "ctx", None),
        P("dp", "ctx", None),
        P("dp", "ctx", None),
        P("dp", "ctx"),
    )
    out_specs = (P("dp", "ctx", None), P("dp", "ctx", None), P("dp", "ctx", None), P())
    return jax.shard_map(body, mesh=mesh, in_specs=in_specs, out_specs=out_specs, check_vma=False)
```
